32 devices in a mesh: dp: 4 (over y, core), expert: 8 (over z, x).
Axes of the slice: x: 2, y: 2, z: 4, core: 2. Of those that a mesh axis runs over, the one named last changes fastest.
Arguments:
- tokens: bfloat16 [2, 512, 3584], P(None, ('dp', 'expert')), parts along dimension 1, may hold values from -6 to 6
- expert_ids: int32 [2, 512, 2], P(None, ('dp', 'expert')), parts along dimension 1, may hold values from 0 to 3, as said below
- route_weights: float32 [2, 512, 2], P(None, ('dp', 'expert')), parts along dimension 1, may hold values from 0.4 to 2
- owner_map: int32 [16], P('dp'), parts along dimension 0, may hold values from 0 to 3, each once
- expert_weights: bfloat16 [4096, 3, 3584], P('expert'), may hold values from -0.09375 to 0.09375
Outputs:
- mixed: bfloat16 [2, 512, 3584], P(None, ('dp', 'expert')), parts along dimension 1
The draws below stay inside these ranges and needn't reach their ends.
There are 4 independent parts, one for each index of `dp`. The reference program is written for one: setup_inputs(seed, part) draws one part's arguments, and reference() takes and returns one part's arrays. A program takes and returns all parts, laid end to end along the dimension named above; an argument that names none is the same for every part. Nothing has to cross between parts.
Inputs may be any that keep to these rules, and one draw needn't show every extreme that they name: `expert_ids`: each token names 2 different experts. One expert, the same for all steps and devices of a part, is named by at least 8 of the tokens of every device in every step, by all 16 tokens of some device in some step, and by more of the tokens of every device over the 2 steps together than any other expert; every other expert is named by at most 8 tokens of one device in one step, a bound reached in every draw. `owner_map`: each group owns exactly one expert.
All inputs are finite; a program needn't handle non-finite values.
Results may differ from the reference program's by a relative error of at most 0.006.
Values may be sent and summed in bfloat16 or wider, within the bound.
A program may use at most 64 MiB of HBM per device.

```python
import jax
import jax.numpy as jnp
from jax import lax

D = 3584
HIDDEN_SIZE = 1024
EXPERTS = 4
TOP = 2
STEPS = 2
ROWS = 16
TOKENS = 128
N_EXPERT = 8


def draw_expert_ids(key, part):
    block_count = STEPS * (TOKENS // ROWS)
    subkeys = jax.random.split(jax.random.fold_in(key, 23), 6)
    hot_expert = jax.random.randint(subkeys[0], (), 0, EXPERTS)
    lacking = jax.random.randint(subkeys[1], (block_count,), 0, ROWS // 2)
    first_block = jax.random.randint(subkeys[2], (), 0, block_count)
    block_index = jnp.arange(block_count)
    lacking = jnp.where(block_index == first_block, ROWS // 2, lacking)
    lacking = jnp.where(block_index == (first_block + 1) % block_count, 0, lacking)
    orders = jax.vmap(lambda subkey: jax.random.permutation(subkey, ROWS))(jax.random.split(subkeys[3], block_count))
    lacks_hot = orders < lacking[:, None]
    consumed = jnp.where(lacks_hot, 2, 1)
    start_slot = jnp.cumsum(consumed, axis=1) - consumed
    offsets = jax.random.randint(subkeys[4], (block_count, 1), 0, EXPERTS - 1)
    first_cold = (hot_expert + 1 + (offsets + start_slot) % (EXPERTS - 1)) % EXPERTS
    second_cold = (hot_expert + 1 + (offsets + start_slot + 1) % (EXPERTS - 1)) % EXPERTS
    pick_first = jnp.where(lacks_hot, first_cold, hot_expert)
    pick_second = jnp.where(lacks_hot, second_cold, first_cold)
    flipped = jax.random.randint(subkeys[5], (block_count, ROWS), 0, 2) == 1
    leading = jnp.where(flipped, pick_second, pick_first)
    trailing = jnp.where(flipped, pick_first, pick_second)
    return jnp.stack([leading, trailing], axis=-1).reshape(STEPS, TOKENS, TOP).astype(jnp.int32)


def block_levels(rng, dims, shards, least, high):
    def one(axis_at, parts):
        draws = jax.random.uniform(jax.random.fold_in(jax.random.fold_in(rng, 6), axis_at), (parts,), jnp.float32, least / len(shards), high / len(shards))
        return jnp.repeat(jnp.exp(draws), dims[axis_at] // parts).reshape((-1,) + (1,) * (len(dims) - axis_at - 1))

    factor_of = one(*shards[0])
    for cut in shards[1:]:
        factor_of = factor_of * one(*cut)
    return factor_of


def bell_draw(key, extent, width, most, shards=(), dtype=jnp.bfloat16):
    factor_of = block_levels(key, extent, shards, -0.22, 0.18) if shards else 1.0
    result = jax.random.normal(key, extent, jnp.float32) * width * factor_of
    return jnp.minimum(jnp.maximum(result, -most), most).astype(dtype)


def setup_inputs(seed: int = 0, part: int = 0) -> dict:
    key_of = jax.random.split(jax.random.key(seed), 6)
    own_keys = jax.random.split(jax.random.fold_in(key_of[5], part), 6)
    tokens = bell_draw(own_keys[0], (STEPS, TOKENS, D), 1.0, 6.0, ((1, 8),))
    expert_ids = draw_expert_ids(jax.random.fold_in(jax.random.fold_in(key_of[5], part), 71), part)
    route_weights = jnp.clip(0.4 + 1.6 * jax.random.uniform(own_keys[2], (STEPS, TOKENS, TOP), jnp.float32) ** block_levels(own_keys[2], (STEPS, TOKENS, TOP), ((1, 8),), -0.2, 0.2), 0.4, 2.0)
    owner_map = jax.random.permutation(own_keys[3], EXPERTS).astype(jnp.int32)
    expert_weights = bell_draw(key_of[4], (EXPERTS * HIDDEN_SIZE, 3, D), D ** -0.5, 0.09375, ((0, 8),))
    return {"tokens": tokens, "expert_ids": expert_ids, "route_weights": route_weights, "owner_map": owner_map, "expert_weights": expert_weights}


def reference(tokens, expert_ids, route_weights, owner_map, expert_weights):
    copies = N_EXPERT // EXPERTS
    slice_width = HIDDEN_SIZE // copies
    flat_tokens = tokens.reshape(-1, D)
    flat_ids = expert_ids.reshape(-1, TOP)
    flat_route = route_weights.reshape(-1, TOP)
    running_sum = jnp.zeros((flat_tokens.shape[0], D), jnp.float32)
    for group_index in range(EXPERTS):
        owned_expert = jnp.sum(jnp.where(owner_map == group_index, jnp.arange(EXPERTS).astype(jnp.int32), 0)).astype(jnp.int32)
        group_weights = expert_weights[group_index * HIDDEN_SIZE:(group_index + 1) * HIDDEN_SIZE]
        gate = jnp.dot(flat_tokens, group_weights[:, 0, :].T, preferred_element_type=jnp.float32)
        upward = jnp.dot(flat_tokens, group_weights[:, 1, :].T, preferred_element_type=jnp.float32)
        hidden = (jax.nn.silu(gate) * upward).astype(jnp.bfloat16)
        slice_parts = jnp.einsum("nkh,khd->nkd", hidden.reshape(-1, copies, slice_width).astype(jnp.float32),
                                 group_weights[:, 2, :].reshape(copies, slice_width, D).astype(jnp.float32),
                                 precision=lax.Precision.HIGHEST)
        rounded = lax.optimization_barrier(slice_parts.astype(jnp.bfloat16))
        expert_out = jnp.sum(rounded.astype(jnp.float32), axis=1)
        coefficient = jnp.sum(jnp.where(flat_ids == owned_expert, flat_route, 0.0), axis=1)
        running_sum = running_sum + coefficient[:, None] * expert_out
    return running_sum.astype(jnp.bfloat16).reshape(tokens.shape)
```

```python
import functools

import jax
import jax.numpy as jnp
from jax import lax
from jax.experimental import pallas as pl
from jax.experimental.pallas import tpu as pltpu
from jax.sharding import PartitionSpec as P

LANES = 128
PIECES = 2


def kernel(groups, copies, x_ref, ext_ref, w_ref, out_ref, w_buf, got, part, from_minor, joined, from_major,
           w_sem, gs_sem, gr_sem, ms_sem, mr_sem, zs_sem, zr_sem):
    steps, rows, width = x_ref.shape
    units = w_ref.shape[1]
    me = lax.axis_index("expert")
    m, c = me // copies, me % copies
    total_rows = groups * copies * rows
    piece = width // PIECES
    majors = [(m + 1 - 2 * (m % 2)), (m + 2) % groups, groups - 1 - m]
    minors = [(c + j) % copies for j in range(1, copies)]

    loads = [pltpu.make_async_copy(w_ref.at[i], w_buf.at[i], w_sem.at[i]) for i in range(3)]
    for load in loads:
        load.start()
    for s in range(steps):
        got[s, me, :, :width] = x_ref[s]
        got[s, me, :, width:] = ext_ref[s]

    barrier = pltpu.get_barrier_semaphore()
    for mp in majors:
        pl.semaphore_signal(barrier, inc=1, device_id={"expert": mp * copies + c}, device_id_type=pl.DeviceIdType.MESH)
    for cp in minors:
        pl.semaphore_signal(barrier, inc=1, device_id={"expert": m * copies + cp}, device_id_type=pl.DeviceIdType.MESH)
    pl.semaphore_wait(barrier, len(majors) + len(minors))

    sends = []

    def remote(src, dst, send_sem, recv_sem, target):
        return pltpu.make_async_remote_copy(src_ref=src, dst_ref=dst, send_sem=send_sem, recv_sem=recv_sem,
                                            device_id={"expert": target}, device_id_type=pl.DeviceIdType.MESH)

    def gather_major(s, k):
        copy = remote(got.at[s, me], got.at[s, me], gs_sem.at[s, k], gr_sem.at[s, k], majors[k] * copies + c)
        copy.start()
        sends.append(copy)

    def gather_wait_major(s, k):
        slot = got.at[s, majors[k] * copies + c]
        remote(slot, slot, gs_sem.at[s, k], gr_sem.at[s, k], majors[k] * copies + c).wait_recv()

    def route(k, j):
        return len(majors) + (k + 1) * len(minors) + j

    def relay(s, k):
        home = m if k < 0 else majors[k]
        slot = got.at[s, home * copies + c]
        for j, cp in enumerate(minors):
            q = route(k, j)
            copy = remote(slot, slot, gs_sem.at[s, q], gr_sem.at[s, q], m * copies + cp)
            copy.start()
            sends.append(copy)

    def relay_wait(s):
        for k in range(-1, len(majors)):
            home = m if k < 0 else majors[k]
            for j in range(len(minors)):
                q = route(k, j)
                origin = (c + copies - (j + 1)) % copies
                slot = got.at[s, home * copies + origin]
                remote(slot, slot, gs_sem.at[s, q], gr_sem.at[s, q], m * copies + origin).wait_recv()

    def hidden_of(s, between):
        block = min(256, units)
        hs = []
        x = got[s, :, :, :width].reshape(total_rows, width)
        for i in range(units // block):
            cut = pl.ds(i * block, block)
            dims = (((1,), (1,)), ((), ()))
            gate = lax.dot_general(x, w_buf[0, cut, :], dims, preferred_element_type=jnp.float32)
            up = lax.dot_general(x, w_buf[1, cut, :], dims, preferred_element_type=jnp.float32)
            hs.append((jax.nn.silu(gate) * up).astype(jnp.bfloat16))
            if i == 0:
                between()
        return jnp.concatenate(hs, axis=1) if len(hs) > 1 else hs[0]

    def scale_of(s):
        ext = got[s, :, :, width:].reshape(total_rows, LANES).astype(jnp.float32)
        lane = lax.broadcasted_iota(jnp.int32, ext.shape, 1)
        mine = (lane % groups == m) & (lane < 3 * groups)
        return jnp.sum(jnp.where(mine, ext, 0.0), axis=1, keepdims=True)

    def down(s, hidden, scale):
        for p in range(PIECES):
            cut = pl.ds(p * piece, piece)
            y = jnp.dot(hidden, w_buf[2, :, cut], preferred_element_type=jnp.float32)
            part[s, :, :, :, cut] = (y * scale).astype(jnp.bfloat16).reshape(groups, copies, rows, piece)
            for j, cp in enumerate(minors):
                copy = remote(part.at[s, :, cp, :, cut], from_minor.at[s, c, :, :, cut],
                              ms_sem.at[s, p, j], mr_sem.at[s, p, j], m * copies + cp)
                copy.start()
                sends.append(copy)

    def join(s):
        for p in range(PIECES):
            cut = pl.ds(p * piece, piece)
            total = part[s, :, c, :, cut].astype(jnp.float32)
            for j in range(len(minors)):
                origin = (c + copies - (j + 1)) % copies
                landed = from_minor.at[s, origin, :, :, cut]
                remote(landed, landed, ms_sem.at[s, p, j], mr_sem.at[s, p, j], m * copies + origin).wait_recv()
                total += from_minor[s, origin, :, :, cut].astype(jnp.float32)
            joined[s, :, :, cut] = total.astype(jnp.bfloat16)
            for k, mp in enumerate(majors):
                copy = remote(joined.at[s, mp, :, cut], from_major.at[s, m, :, cut],
                              zs_sem.at[s, p, k], zr_sem.at[s, p, k], mp * copies + c)
                copy.start()
                sends.append(copy)

    def finish(s):
        for p in range(PIECES):
            cut = pl.ds(p * piece, piece)
            total = joined[s, m, :, cut].astype(jnp.float32)
            for k, mp in enumerate(majors):
                landed = from_major.at[s, mp, :, cut]
                remote(landed, landed, zs_sem.at[s, p, k], zr_sem.at[s, p, k], mp * copies + c).wait_recv()
                total += from_major[s, mp, :, cut].astype(jnp.float32)
            out_ref[s, :, cut] = total.astype(out_ref.dtype)

    for s in range(steps):
        relay(s, -1)
        for k in range(len(majors)):
            gather_major(s, k)

    def forward(s):
        for k in range(len(majors)):
            gather_wait_major(s, k)
            relay(s, k)

    forward(0)
    for s in range(steps):
        relay_wait(s)
        if s == 0:
            loads[0].wait()
            loads[1].wait()

        def between(s=s):
            if s + 1 < steps:
                forward(s + 1)

        hidden = hidden_of(s, between)
        if s == 0:
            loads[2].wait()
        else:
            join(s - 1)
        down(s, hidden, scale_of(s))
    join(steps - 1)
    for s in range(steps):
        finish(s)
    for copy in sends:
        copy.wait_send()


def shards(tokens, expert_ids, route_weights, owner_map, expert_weights):
    device_count = lax.axis_size("expert")
    groups = owner_map.shape[0]
    copies = device_count // groups
    steps, rows, width = tokens.shape
    units = expert_weights.shape[0]
    weights = jnp.transpose(expert_weights, (1, 0, 2))

    expert_range = jnp.arange(groups, dtype=jnp.int32)
    owner = jnp.sum(jnp.where(expert_ids[..., None] == expert_range, owner_map, 0), axis=-1)
    lane = jnp.arange(LANES, dtype=jnp.int32)
    coefficient = jnp.sum(
        jnp.where(owner[..., None] == lane % groups, route_weights[..., None], 0.0), axis=2
    )
    high = lax.reduce_precision(coefficient, 8, 7)
    middle = lax.reduce_precision(coefficient - high, 8, 7)
    low = coefficient - high - middle
    ext = jnp.where(lane < groups, high, jnp.where(lane < 2 * groups, middle, jnp.where(lane < 3 * groups, low, 0.0)))
    ext = ext.astype(jnp.bfloat16)

    routes = (groups - 1) + groups * (copies - 1)
    vmem = pl.BlockSpec(memory_space=pltpu.VMEM)
    dma = pltpu.SemaphoreType.DMA
    return pl.pallas_call(
        functools.partial(kernel, groups, copies),
        out_shape=jax.ShapeDtypeStruct((steps, rows, width), jnp.bfloat16),
        in_specs=[vmem, vmem, pl.BlockSpec(memory_space=pl.ANY)],
        out_specs=vmem,
        scratch_shapes=[
            pltpu.VMEM((3, units, width), jnp.bfloat16),
            pltpu.VMEM((steps, device_count, rows, width + LANES), jnp.bfloat16),
            pltpu.VMEM((steps, groups, copies, rows, width), jnp.bfloat16),
            pltpu.VMEM((steps, copies, groups, rows, width), jnp.bfloat16),
            pltpu.VMEM((steps, groups, rows, width), jnp.bfloat16),
            pltpu.VMEM((steps, groups, rows, width), jnp.bfloat16),
            dma((3,)),
            dma((steps, routes)),
            dma((steps, routes)),
            dma((steps, PIECES, copies - 1)),
            dma((steps, PIECES, copies - 1)),
            dma((steps, PIECES, groups - 1)),
            dma((steps, PIECES, groups - 1)),
        ],
        compiler_params=pltpu.CompilerParams(
            collective_id=0, has_side_effects=True, vmem_limit_bytes=56 * 1024 * 1024
        ),
    )(tokens, ext, weights)


def solution(mesh):
    placed = (
        P(None, ("dp", "expert"), None),
        P(None, ("dp", "expert"), None),
        P(None, ("dp", "expert"), None),
        P("dp"),
        P("expert", None, None),
    )
    return jax.shard_map(
        shards,
        mesh=mesh,
        in_specs=placed,
        out_specs=P(None, ("dp", "expert"), None),
        check_vma=False,
    )
```

```python
import functools

import jax
import jax.numpy as jnp
from jax import lax
from jax.experimental import pallas as pl
from jax.experimental.pallas import tpu as pltpu
from jax.sharding import PartitionSpec as P

LANES = 128
PIECES = 4


def coefficients(groups, rows, ids, route, owner_ref):
    diagonal = lax.broadcasted_iota(jnp.int32, (rows, rows), 0) == lax.broadcasted_iota(jnp.int32, (rows, rows), 1)
    lane = lax.broadcasted_iota(jnp.int32, (rows, LANES), 1)
    group = (lane % groups).astype(jnp.float32)
    total = jnp.zeros((rows, LANES), jnp.float32)
    for k in range(ids.shape[0]):
        owner = jnp.zeros((1, rows), jnp.float32)
        for e in range(groups):
            owner += jnp.where(ids[k:k + 1] == e, owner_ref[e].astype(jnp.float32), 0.0)
        owner = jnp.sum(jnp.where(diagonal, owner, 0.0), axis=1, keepdims=True)
        weight = jnp.sum(jnp.where(diagonal, route[k:k + 1], 0.0), axis=1, keepdims=True)
        total += jnp.where(owner == group, weight, 0.0)
    high = total.astype(jnp.bfloat16).astype(jnp.float32)
    middle = (total - high).astype(jnp.bfloat16).astype(jnp.float32)
    low = total - high - middle
    ext = jnp.where(lane < groups, high, jnp.where(lane < 2 * groups, middle, jnp.where(lane < 3 * groups, low, 0.0)))
    return ext.astype(jnp.bfloat16)


def kernel(groups, copies, x_ref, ids_ref, route_ref, owner_ref, w_ref, out_ref, w_buf, got, part, from_minor, joined, from_major,
           w_sem, gs_sem, gr_sem, ms_sem, mr_sem, zs_sem, zr_sem):
    steps, rows, width = x_ref.shape
    units = w_ref.shape[1]
    me = lax.axis_index("expert")
    m, c = me // copies, me % copies
    total_rows = groups * copies * rows
    piece = width // PIECES
    majors = [(m + 1 - 2 * (m % 2)), (m + 2) % groups, groups - 1 - m]
    minors = [(c + j) % copies for j in range(1, copies)]

    loads = [pltpu.make_async_copy(w_ref.at[i], w_buf.at[i], w_sem.at[i]) for i in range(3)]
    for load in loads:
        load.start()
    for s in range(steps):
        got[s, me, :, :width] = x_ref[s]
        got[s, me, :, width:] = coefficients(groups, rows, ids_ref[s], route_ref[s], owner_ref)

    barrier = pltpu.get_barrier_semaphore()
    for mp in majors:
        pl.semaphore_signal(barrier, inc=1, device_id={"expert": mp * copies + c}, device_id_type=pl.DeviceIdType.MESH)
    for cp in minors:
        pl.semaphore_signal(barrier, inc=1, device_id={"expert": m * copies + cp}, device_id_type=pl.DeviceIdType.MESH)
    pl.semaphore_wait(barrier, len(majors) + len(minors))

    sends = []

    def remote(src, dst, send_sem, recv_sem, target):
        return pltpu.make_async_remote_copy(src_ref=src, dst_ref=dst, send_sem=send_sem, recv_sem=recv_sem,
                                            device_id={"expert": target}, device_id_type=pl.DeviceIdType.MESH)

    def gather_major(s, k):
        copy = remote(got.at[s, me], got.at[s, me], gs_sem.at[s, k], gr_sem.at[s, k], majors[k] * copies + c)
        copy.start()
        sends.append(copy)

    def gather_wait_major(s, k):
        slot = got.at[s, majors[k] * copies + c]
        remote(slot, slot, gs_sem.at[s, k], gr_sem.at[s, k], majors[k] * copies + c).wait_recv()

    def route(k, j):
        return len(majors) + (k + 1) * len(minors) + j

    def relay(s, k):
        home = m if k < 0 else majors[k]
        slot = got.at[s, home * copies + c]
        for j, cp in enumerate(minors):
            q = route(k, j)
            copy = remote(slot, slot, gs_sem.at[s, q], gr_sem.at[s, q], m * copies + cp)
            copy.start()
            sends.append(copy)

    def relay_wait(s):
        for k in range(-1, len(majors)):
            home = m if k < 0 else majors[k]
            for j in range(len(minors)):
                q = route(k, j)
                origin = (c + copies - (j + 1)) % copies
                slot = got.at[s, home * copies + origin]
                remote(slot, slot, gs_sem.at[s, q], gr_sem.at[s, q], m * copies + origin).wait_recv()

    def hidden_of(s, between):
        block = min(256, units)
        hs = []
        x = got[s, :, :, :width].reshape(total_rows, width)
        for i in range(units // block):
            cut = pl.ds(i * block, block)
            dims = (((1,), (1,)), ((), ()))
            gate = lax.dot_general(x, w_buf[0, cut, :], dims, preferred_element_type=jnp.float32)
            up = lax.dot_general(x, w_buf[1, cut, :], dims, preferred_element_type=jnp.float32)
            hs.append((jax.nn.silu(gate) * up).astype(jnp.bfloat16))
            if i == 0:
                between()
        return jnp.concatenate(hs, axis=1) if len(hs) > 1 else hs[0]

    def scale_of(s):
        ext = got[s, :, :, width:].reshape(total_rows, LANES).astype(jnp.float32)
        lane = lax.broadcasted_iota(jnp.int32, ext.shape, 1)
        mine = (lane % groups == m) & (lane < 3 * groups)
        return jnp.sum(jnp.where(mine, ext, 0.0), axis=1, keepdims=True)

    def down(s, hidden, scale):
        for p in range(PIECES):
            cut = pl.ds(p * piece, piece)
            y = jnp.dot(hidden, w_buf[2, :, cut], preferred_element_type=jnp.float32)
            part[s, :, :, :, cut] = (y * scale).astype(jnp.bfloat16).reshape(groups, copies, rows, piece)
            for j, cp in enumerate(minors):
                copy = remote(part.at[s, :, cp, :, cut], from_minor.at[s, c, :, :, cut],
                              ms_sem.at[s, p, j], mr_sem.at[s, p, j], m * copies + cp)
                copy.start()
                sends.append(copy)

    def join(s):
        for p in range(PIECES):
            cut = pl.ds(p * piece, piece)
            total = part[s, :, c, :, cut].astype(jnp.float32)
            for j in range(len(minors)):
                origin = (c + copies - (j + 1)) % copies
                landed = from_minor.at[s, origin, :, :, cut]
                remote(landed, landed, ms_sem.at[s, p, j], mr_sem.at[s, p, j], m * copies + origin).wait_recv()
                total += from_minor[s, origin, :, :, cut].astype(jnp.float32)
            joined[s, :, :, cut] = total.astype(jnp.bfloat16)
            for k, mp in enumerate(majors):
                copy = remote(joined.at[s, mp, :, cut], from_major.at[s, m, :, cut],
                              zs_sem.at[s, p, k], zr_sem.at[s, p, k], mp * copies + c)
                copy.start()
                sends.append(copy)

    def finish(s):
        for p in range(PIECES):
            cut = pl.ds(p * piece, piece)
            total = joined[s, m, :, cut].astype(jnp.float32)
            for k, mp in enumerate(majors):
                landed = from_major.at[s, mp, :, cut]
                remote(landed, landed, zs_sem.at[s, p, k], zr_sem.at[s, p, k], mp * copies + c).wait_recv()
                total += from_major[s, mp, :, cut].astype(jnp.float32)
            out_ref[s, :, cut] = total.astype(out_ref.dtype)

    for s in range(steps):
        relay(s, -1)
        for k in range(len(majors)):
            gather_major(s, k)

    def forward(s):
        for k in range(len(majors)):
            gather_wait_major(s, k)
            relay(s, k)

    forward(0)
    for s in range(steps):
        relay_wait(s)
        if s == 0:
            loads[0].wait()
            loads[1].wait()

        def between(s=s):
            if s + 1 < steps:
                forward(s + 1)

        hidden = hidden_of(s, between)
        if s == 0:
            loads[2].wait()
        else:
            join(s - 1)
        down(s, hidden, scale_of(s))
    join(steps - 1)
    for s in range(steps):
        finish(s)
    for copy in sends:
        copy.wait_send()


def shards(tokens, expert_ids, route_weights, owner_map, expert_weights):
    device_count = lax.axis_size("expert")
    groups = owner_map.shape[0]
    copies = device_count // groups
    steps, rows, width = tokens.shape
    units = expert_weights.shape[0]
    weights = jnp.transpose(expert_weights, (1, 0, 2))

    routes = (groups - 1) + groups * (copies - 1)
    vmem = pl.BlockSpec(memory_space=pltpu.VMEM)
    dma = pltpu.SemaphoreType.DMA
    return pl.pallas_call(
        functools.partial(kernel, groups, copies),
        out_shape=jax.ShapeDtypeStruct((steps, rows, width), jnp.bfloat16),
        in_specs=[vmem, vmem, vmem, pl.BlockSpec(memory_space=pltpu.SMEM), pl.BlockSpec(memory_space=pl.ANY)],
        out_specs=vmem,
        scratch_shapes=[
            pltpu.VMEM((3, units, width), jnp.bfloat16),
            pltpu.VMEM((steps, device_count, rows, width + LANES), jnp.bfloat16),
            pltpu.VMEM((steps, groups, copies, rows, width), jnp.bfloat16),
            pltpu.VMEM((steps, copies, groups, rows, width), jnp.bfloat16),
            pltpu.VMEM((steps, groups, rows, width), jnp.bfloat16),
            pltpu.VMEM((steps, groups, rows, width), jnp.bfloat16),
            dma((3,)),
            dma((steps, routes)),
            dma((steps, routes)),
            dma((steps, PIECES, copies - 1)),
            dma((steps, PIECES, copies - 1)),
            dma((steps, PIECES, groups - 1)),
            dma((steps, PIECES, groups - 1)),
        ],
        compiler_params=pltpu.CompilerParams(
            collective_id=0, has_side_effects=True, vmem_limit_bytes=56 * 1024 * 1024
        ),
    )(
        tokens, jnp.transpose(expert_ids, (0, 2, 1)), jnp.transpose(route_weights, (0, 2, 1)), owner_map, weights
    )


def solution(mesh):
    placed = (
        P(None, ("dp", "expert"), None),
        P(None, ("dp", "expert"), None),
        P(None, ("dp", "expert"), None),
        P("dp"),
        P("expert", None, None),
    )
    return jax.shard_map(
        shards,
        mesh=mesh,
        in_specs=placed,
        out_specs=P(None, ("dp", "expert"), None),
        check_vma=False,
    )
```
